256 devices in a mesh: replica: 64 (over x, z_hi, y, core), tensor: 4 (over z_lo).
Axes of the slice: x: 4, y: 4, z: 8 (z_hi: 2, z_lo: 4; z = z_hi * 4 + z_lo), core: 2. Of those that a mesh axis runs over, the one named last changes fastest.
Arguments:
- history: bfloat16 [3584, 2, 64, 512], P('replica', None, None, 'tensor')
- new_queries: bfloat16 [3584, 32, 4096], P('replica', 'tensor')
- new_kv: bfloat16 [3584, 32, 4, 2, 128], P('replica', 'tensor'), may hold values from -6 to 6
- norm_gains: bfloat16 [2, 128], replicated, may hold values from 0.5 to 2
- ingest_source: int32 [64], replicated, may hold values from 0 to 63, each once
- new_owner: int32 [3584, 1], replicated, may hold values from 0 to 63, as said below
- history_len: int32 [3584], replicated, may hold values from 1 to 64
- new_len: int32 [3584], replicated, may hold values from 1 to 32
Outputs:
- attended: bfloat16 [3584, 32, 4096], P('replica', 'tensor')
- migrated: bfloat16 [3584, 2, 96, 512], P('replica', None, None, 'tensor')
The draws below stay inside these ranges and needn't reach their ends.
Inputs may be any that keep to these rules, and one draw needn't show every extreme that they name: Replica j ingests the blocks of the sessions held by replica ingest_source[j], in the same order. `new_owner`: every replica owns exactly 56 sessions after the rebalance. Of the 56 sessions held by one replica (aligned blocks of 56 rows), at most 2 go to any one replica; every replica sends exactly 2 to some replica and receives exactly 2 from some replica, and every replica sends and receives the same counts, in different orders.
All inputs are finite; a program needn't handle non-finite values.
Results may differ from the reference program's by a relative error of at most 0.0078.
Values may be sent and summed in bfloat16 or wider, within the bound.
No kernel may reach another device: no remote copies, remote signals or barrier semaphores. Data moves between devices by JAX's collectives and lax.ppermute only.
A program may use at most 128 MiB of HBM per device.

```python
import math
import jax
import jax.numpy as jnp
from jax import lax

HEAD = 128
KVH = 4
GROUP = 8
S_DEV = 56
HIST = 64
NEW = 32
SESS = 3584
CAP = 2
N_REPLICA = 64


def draw_history(key, part):
    key = jax.random.fold_in(key, 3)
    base_draw = jax.random.normal(key, (SESS, 2, HIST, KVH, HEAD), jnp.float32)
    return base_draw.reshape(SESS, 2, HIST, KVH * HEAD).astype(jnp.bfloat16)


def draw_new_queries(key, part):
    key = jax.random.fold_in(key, 5)
    key_base, key_rows, key_cols = jax.random.split(key, 3)
    shape_full = (SESS, NEW, KVH, GROUP, HEAD)
    base_draw = jax.random.normal(key_base, shape_full, jnp.float32)
    row_scale = jnp.exp(jax.random.uniform(key_rows, (SESS, NEW, KVH, GROUP, 1), jnp.float32, 0.0, math.log(10.0)))
    col_scale = jnp.exp(jax.random.uniform(key_cols, (HEAD,), jnp.float32, math.log(0.5), math.log(5.0)))
    queries = base_draw * row_scale * col_scale
    return queries.reshape(SESS, NEW, KVH * GROUP * HEAD).astype(jnp.bfloat16)


def draw_new_owner(key, part):
    key = jax.random.fold_in(key, 11)
    key_outer, key_inner, key_pick, key_rest, key_rows = jax.random.split(key, 5)
    outer_order = jax.random.permutation(key_outer, N_REPLICA).astype(jnp.int32)
    inner_order = jax.random.permutation(key_inner, N_REPLICA).astype(jnp.int32)
    common = jax.random.randint(key_pick, (), 0, N_REPLICA, jnp.int32)
    spread = (common + 1 + jnp.arange((N_REPLICA - 1) * CAP, dtype=jnp.int32) // CAP) % N_REPLICA
    spread = jax.random.permutation(key_rest, spread)
    offsets = jnp.concatenate([jnp.full((CAP,), common, jnp.int32), spread[:S_DEV - CAP]])

    def shuffle_row(row_key):
        return jax.random.permutation(row_key, offsets)
    shuffled = jax.vmap(shuffle_row)(jax.random.split(key_rows, N_REPLICA))
    owners = inner_order[(outer_order[:, None] + shuffled) % N_REPLICA]
    return owners.reshape(SESS, 1).astype(jnp.int32)


def draw_history_len(key, part):
    key = jax.random.fold_in(key, 7)
    key_vals, key_pick = jax.random.split(key)
    lengths = jax.random.randint(key_vals, (SESS,), 1, HIST + 1, jnp.int32)
    return lengths.at[jax.random.randint(key_pick, (), 0, SESS, jnp.int32)].set(HIST)


def draw_new_len(key, part):
    key = jax.random.fold_in(key, 9)
    key_vals, key_pick = jax.random.split(key)
    lengths = jax.random.randint(key_vals, (SESS,), 1, NEW + 1, jnp.int32)
    return lengths.at[jax.random.randint(key_pick, (), 0, SESS, jnp.int32)].set(NEW)


def level_of(key, extent, pieces, smallest, high):
    level = 1.0
    for dim, shards_of in pieces:
        draws = jax.random.uniform(jax.random.fold_in(jax.random.fold_in(key, 6), dim), (shards_of,), jnp.float32, smallest / len(pieces), high / len(pieces))
        level = level * jnp.repeat(jnp.exp(draws), extent[dim] // shards_of).reshape((-1,) + (1,) * (len(extent) - 1 - dim))
    return level


def centred(key, extent, scale, bound, cuts=(), held_as=jnp.bfloat16):
    values = scale * jax.random.normal(key, extent, jnp.float32)
    if cuts:
        values = values * level_of(key, extent, cuts, -0.22, 0.18)
    return jnp.clip(values, -bound, bound).astype(held_as)


def setup_inputs(seed: int = 0) -> dict:
    streams_of = jax.random.split(jax.random.key(seed), 9)
    history = draw_history(jax.random.fold_in(streams_of[8], 71), 0)
    new_queries = draw_new_queries(jax.random.fold_in(streams_of[8], 71), 0)
    new_kv = centred(streams_of[2], (SESS, NEW, KVH, 2, HEAD), 1.0, 6.0, ((0, 64), (1, 4)))
    norm_gains = jnp.clip(jnp.exp(jax.random.uniform(streams_of[3], (2, HEAD), jnp.float32, math.log(0.5), math.log(2.0))), 0.5, 2.0).astype(jnp.bfloat16)
    ingest_source = jax.random.permutation(streams_of[4], N_REPLICA).astype(jnp.int32)
    new_owner = draw_new_owner(jax.random.fold_in(streams_of[8], 71), 0)
    history_len = draw_history_len(jax.random.fold_in(streams_of[8], 71), 0)
    new_len = draw_new_len(jax.random.fold_in(streams_of[8], 71), 0)
    return {"history": history, "new_queries": new_queries, "new_kv": new_kv, "norm_gains": norm_gains, "ingest_source": ingest_source, "new_owner": new_owner, "history_len": history_len, "new_len": new_len}


def rms_scaled(vectors, scaling):
    mean_square = lax.optimization_barrier(jnp.mean(vectors * vectors, axis=-1, keepdims=True))
    return vectors * lax.rsqrt(mean_square + 1e-06) * scaling

def place_cache(cache, new_keys, new_values, hist_count, new_count):
    positions = jnp.arange(HIST, dtype=jnp.int32)
    tokens = jnp.arange(NEW, dtype=jnp.int32)
    hist_kept = jnp.where((positions < hist_count)[None, :, None], cache, jnp.zeros((), cache.dtype))
    fresh_rows = jnp.stack([new_keys, new_values], axis=0)
    fresh_rows = jnp.where((tokens < new_count)[None, :, None], fresh_rows, jnp.zeros((), fresh_rows.dtype))
    padded = jnp.concatenate([hist_kept, jnp.zeros((2, NEW, cache.shape[2]), cache.dtype)], axis=1)
    zero_index = jnp.zeros((), jnp.int32)
    return lax.dynamic_update_slice(padded, fresh_rows, (zero_index, hist_count.astype(jnp.int32), zero_index))

def reference(history, new_queries, new_kv, norm_gains, ingest_source, new_owner, history_len, new_len):
    score_scale = HEAD ** (-0.5)
    query_heads = KVH * GROUP
    norm_scale = norm_gains.astype(jnp.float32)
    positions = jnp.arange(HIST, dtype=jnp.int32)
    tokens = jnp.arange(NEW, dtype=jnp.int32)
    block_ids = jnp.arange(SESS, dtype=jnp.int32)
    block_session = (ingest_source[block_ids // S_DEV] * S_DEV + block_ids % S_DEV).astype(jnp.int32)
    owners = new_owner[:, 0].astype(jnp.int32)
    owner_hits = (owners[:, None] == jnp.arange(N_REPLICA, dtype=jnp.int32)[None, :]).astype(jnp.int32)
    owner_slot = lax.optimization_barrier(jnp.sum((jnp.cumsum(owner_hits, axis=0) - owner_hits) * owner_hits, axis=1)).astype(jnp.int32)
    cache_row = (owners * S_DEV + owner_slot).astype(jnp.int32)
    row_session = jnp.zeros((SESS,), jnp.int32).at[cache_row].set(block_ids)
    session_block = jnp.zeros((SESS,), jnp.int32).at[block_session].set(block_ids)

    def one_block(block_index):
        session = block_session[block_index]
        query_float = new_queries[block_index].astype(jnp.float32).reshape(NEW, KVH, GROUP, HEAD)
        query_normed = rms_scaled(query_float, norm_scale[0]).astype(jnp.bfloat16)
        new_pairs = new_kv[block_index]
        key_normed = rms_scaled(new_pairs[:, :, 0, :].astype(jnp.float32), norm_scale[1]).astype(jnp.bfloat16)
        hist_keys = history[session, 0].reshape(HIST, KVH, HEAD)
        hist_values = history[session, 1].reshape(HIST, KVH, HEAD)
        all_keys = jnp.concatenate([hist_keys, key_normed], axis=0).astype(jnp.float32)
        all_values = jnp.concatenate([hist_values, new_pairs[:, :, 1, :]], axis=0).astype(jnp.float32)
        scores = jnp.einsum('tkhd,pkd->khtp', query_normed.astype(jnp.float32), all_keys) * score_scale
        hist_mask = positions < history_len[session]
        new_mask = tokens[None, :] <= tokens[:, None]
        allowed = jnp.concatenate([jnp.broadcast_to(hist_mask[None, :], (NEW, HIST)), new_mask], axis=1)
        scores = jnp.where(allowed[None, None], scores, -jnp.inf)
        row_max = lax.optimization_barrier(jnp.max(scores, axis=-1, keepdims=True))
        score_exp = jnp.exp(scores - row_max)
        weights = (score_exp / lax.optimization_barrier(jnp.sum(score_exp, axis=-1, keepdims=True))).astype(jnp.bfloat16)
        mixed_rows = jnp.einsum('khtp,pkd->tkhd', weights.astype(jnp.float32), all_values)
        live_rows = (tokens < new_len[session]).astype(jnp.float32)
        mixed_rows = mixed_rows * live_rows[:, None, None, None]
        return mixed_rows.astype(jnp.bfloat16).reshape(NEW, query_heads * HEAD)

    def one_row(row_index):
        session = row_session[row_index]
        block_index = session_block[session]
        new_pairs = new_kv[block_index]
        key_normed = rms_scaled(new_pairs[:, :, 0, :].astype(jnp.float32), norm_scale[1]).astype(jnp.bfloat16)
        key_flat = key_normed.reshape(NEW, KVH * HEAD)
        value_flat = new_pairs[:, :, 1, :].reshape(NEW, KVH * HEAD)
        return place_cache(history[session], key_flat, value_flat, history_len[session], new_len[session])
    attended = lax.map(one_block, block_ids)
    migrated = lax.map(one_row, block_ids)
    return (attended, migrated)
```

```python
import functools

import jax
import jax.numpy as jnp
from jax import lax
from jax.experimental import pallas as pl
from jax.experimental.pallas import tpu as pltpu
from jax.sharding import Mesh, PartitionSpec as P

REPLICA = ("x", "zh", "y", "core")
SPREAD = ("zh", "x", "y", "core")
COLUMN = ("x", "y", "core")
RING = ("zh", "zl")
CAP = 2
EPS = 1e-06
BF16 = jnp.bfloat16
F32 = jnp.float32


def spread_index(replica):
    x, zh, y, core = replica // 16, (replica // 8) % 2, (replica // 2) % 4, replica % 2
    return zh * 32 + x * 8 + y * 2 + core


def replica_at(spread):
    zh, x, y, core = spread // 32, (spread // 8) % 4, (spread // 2) % 4, spread % 2
    return x * 16 + zh * 8 + y * 2 + core


def attend_kernel(meta, hist_len, new_len, q_ref, k_ref, v_ref, kv_ref, gain_ref, out_ref):
    halves, blocks = pl.program_id(0), pl.program_id(1)
    count, tokens, width = q_ref.shape
    kv_heads, history, head = k_ref.shape[1], k_ref.shape[4], k_ref.shape[5]
    groups = width // (kv_heads * head)
    rows = groups * tokens
    shards = kv_ref.shape[1]
    fresh = shards * tokens
    keys = history + fresh
    first = (halves * pl.num_programs(1) + blocks) * count
    gain = gain_ref[0:1, :].astype(F32)
    scale = head ** (-0.5)
    column = lax.broadcasted_iota(jnp.int32, (rows, keys), 1)
    token = lax.broadcasted_iota(jnp.int32, (rows, keys), 0) % tokens + meta[1] * tokens
    causal = jnp.logical_and(column >= history, column - history <= token)
    out_token = lax.broadcasted_iota(jnp.int32, (rows, head), 0) % tokens + meta[1] * tokens

    def one_session(s, carry):
        length = hist_len[first + s]
        allowed = jnp.logical_or(causal, column < jnp.minimum(length, history))
        live = out_token < new_len[first + s]
        for h in range(kv_heads):
            lanes = [slice((h * groups + g) * head, (h * groups + g + 1) * head) for g in range(groups)]
            query = jnp.concatenate([q_ref[s, :, lane].astype(F32) for lane in lanes], axis=0)
            mean_square = jnp.mean(query * query, axis=-1, keepdims=True)
            query = (query * lax.rsqrt(mean_square + EPS) * gain).astype(BF16)
            fresh_k = [kv_ref[0, i, h, s, 0].astype(F32) for i in range(shards)]
            fresh_v = [kv_ref[0, i, h, s, 1].astype(F32) for i in range(shards)]
            key = jnp.concatenate([k_ref[0, h, 0, s], jnp.concatenate(fresh_k, axis=0).astype(BF16)], axis=0)
            value = jnp.concatenate([v_ref[0, h, 0, s], jnp.concatenate(fresh_v, axis=0).astype(BF16)], axis=0)
            scores = lax.dot_general(query, key, (((1,), (1,)), ((), ())), preferred_element_type=F32) * scale
            scores = jnp.where(allowed, scores, -jnp.inf)
            peak = jnp.max(scores, axis=-1, keepdims=True)
            weight = jnp.exp(scores - peak)
            weight = (weight / jnp.sum(weight, axis=-1, keepdims=True)).astype(BF16)
            mixed = jnp.dot(weight, value, preferred_element_type=F32)
            mixed = jnp.where(live, mixed, 0.0)
            for g, lane in enumerate(lanes):
                out_ref[s, :, lane] = mixed[g * tokens : (g + 1) * tokens].astype(BF16)
        return carry

    lax.fori_loop(0, count, one_session, 0)


def attend(queries, keys, values, fresh, gains, hist_len, new_len, half, shard):
    sessions, tokens, width = queries.shape
    _, kv_heads, _, per_half, history, head = keys.shape
    shards = fresh.shape[1]
    count = per_half // 4
    blocks = per_half // count
    meta = jnp.stack([half, shard]).astype(jnp.int32)
    whole = lambda i, j, m, a, b: (i * blocks + j, 0, 0)
    cached = pl.BlockSpec((1, kv_heads, 1, count, history, head), lambda i, j, m, a, b: (i, 0, m[0], j, 0, 0))
    return pl.pallas_call(
        attend_kernel,
        out_shape=jax.ShapeDtypeStruct(queries.shape, BF16),
        grid_spec=pltpu.PrefetchScalarGridSpec(
            num_scalar_prefetch=3,
            grid=(2, blocks),
            in_specs=[
                pl.BlockSpec((count, tokens, width), whole),
                cached,
                cached,
                pl.BlockSpec(
                    (1, shards, kv_heads, count, 2, tokens, head),
                    lambda i, j, m, a, b: (m[0], 0, 0, i * blocks + j, 0, 0, 0),
                ),
                pl.BlockSpec((2, head), lambda i, j, m, a, b: (0, 0)),
            ],
            out_specs=pl.BlockSpec((count, tokens, width), whole),
        ),
        compiler_params=pltpu.CompilerParams(vmem_limit_bytes=48 * 1024 * 1024),
    )(meta, hist_len, new_len, queries, keys, values, fresh, gains)


def build_kernel(slot_from, hist_len, new_len, k_ref, v_ref, kv_ref, out_ref):
    count, _, rows, head = out_ref.shape
    history = k_ref.shape[1]
    shards, tokens = kv_ref.shape[1], kv_ref.shape[3]
    target_row = lax.broadcasted_iota(jnp.int32, (rows, rows), 0)
    source = lax.broadcasted_iota(jnp.int32, (rows, rows), 1)

    def one_slot(j, carry):
        at, length, live = slot_from[j], hist_len[j], new_len[j]
        moved = jnp.where(source - history < live, source - history + length, -1)
        target = jnp.where(source < history, jnp.where(source < length, source, -1), moved)
        pick = (target_row == target).astype(F32).astype(BF16)
        fresh = [
            jnp.concatenate([kv_ref[at, i, part].astype(F32) for i in range(shards)], axis=0).astype(BF16)
            for part in range(2)
        ]
        key = jnp.concatenate([k_ref[at], fresh[0]], axis=0)
        value = jnp.concatenate([v_ref[at], fresh[1]], axis=0)
        out_ref[j, 0] = jnp.dot(pick, key, preferred_element_type=F32).astype(BF16)
        out_ref[j, 1] = jnp.dot(pick, value, preferred_element_type=F32).astype(BF16)
        return carry

    lax.fori_loop(0, count, one_slot, 0)


def build(keys, values, fresh, slot_from, hist_len, new_len):
    count = slot_from.shape[0]
    history, head = keys.shape[1:]
    rows = history + fresh.shape[1] * fresh.shape[3]
    vmem = pl.BlockSpec(memory_space=pltpu.VMEM)
    smem = pl.BlockSpec(memory_space=pltpu.SMEM)
    return pl.pallas_call(
        build_kernel,
        out_shape=jax.ShapeDtypeStruct((count, 2, rows, head), BF16),
        in_specs=[smem, smem, smem, vmem, vmem, vmem],
        out_specs=vmem,
        compiler_params=pltpu.CompilerParams(vmem_limit_bytes=48 * 1024 * 1024),
    )(slot_from, hist_len, new_len, keys, values, fresh)


def on_device(history, new_queries, new_kv, norm_gains, ingest_source, new_owner, history_len, new_len):
    sessions, _, hist_rows, head = history.shape
    half_sessions = sessions // 2
    tokens, kv_heads = new_kv.shape[1], new_kv.shape[2]
    half, shard = lax.axis_index("zh"), lax.axis_index("zl")
    me = lax.axis_index(REPLICA)
    column = lax.axis_index(COLUMN)

    raw_key = new_kv[:, :, :, 0, :].astype(F32)
    mean_square = jnp.mean(raw_key * raw_key, axis=-1, keepdims=True)
    normed = (raw_key * lax.rsqrt(mean_square + EPS) * norm_gains[1].astype(F32)).astype(BF16)
    fresh = jnp.stack([normed, new_kv[:, :, :, 1, :]], axis=0).transpose(3, 1, 0, 2, 4)
    fresh_all = lax.all_gather(fresh, RING, axis=0).reshape((2, 4) + fresh.shape)

    source_spread = spread_index(ingest_source[replica_at(jnp.arange(64, dtype=jnp.int32))])
    source_order = source_spread.reshape(2, 32).T.reshape(64)

    def collect(part):
        pieces = part.reshape(64, -1, head)
        spread = lax.all_to_all(pieces, SPREAD, split_axis=0, concat_axis=0, tiled=True)
        picked = jnp.take(spread, source_order, axis=0, mode="clip").reshape(32, 2, -1, head)
        held = lax.all_to_all(picked, COLUMN, split_axis=0, concat_axis=1)
        held = held.reshape(2, half_sessions, hist_rows, head)
        return lax.all_gather(held, RING, axis=0).reshape(2, 4, 2, half_sessions, hist_rows, head)

    keys, values = collect(history[:, 0]), collect(history[:, 1])

    owners = new_owner[:, 0].reshape(64, sessions)
    mine = ingest_source[replica_at(jnp.arange(2, dtype=jnp.int32) * 32 + column)]
    mine_owner = owners[mine]
    order = jnp.arange(sessions, dtype=jnp.int32)
    same = mine_owner[:, :, None] == mine_owner[:, None, :]
    rank = jnp.sum(jnp.logical_and(same, order[None, None, :] < order[None, :, None]), axis=2)
    target = replica_at(half * 32 + jnp.arange(32, dtype=jnp.int32))
    hit = jnp.logical_and(
        mine_owner[None, :, None, :] == target[:, None, None, None],
        rank[None, :, None, :] == jnp.arange(CAP)[None, None, :, None],
    )
    chosen = jnp.sum(jnp.where(hit, order, 0), axis=3).reshape(32, 2 * CAP)
    from_half = (jnp.arange(2 * CAP, dtype=jnp.int32) // CAP)[None, :]
    block = ((chosen // half_sessions) * 4 + shard) * 2 + from_half
    cached_at = (block * half_sessions + chosen % half_sessions).reshape(-1)
    fresh_at = (from_half * 4)[:, :, None] + jnp.arange(4, dtype=jnp.int32)
    fresh_at = ((fresh_at * kv_heads + shard) * sessions + chosen[:, :, None]).reshape(-1)

    def deliver(rows, at):
        sent = jnp.take(rows, at, axis=0, mode="clip").reshape((32, -1) + rows.shape[1:])
        return lax.all_to_all(sent, COLUMN, split_axis=0, concat_axis=0, tiled=True)

    fresh_in = deliver(fresh_all.reshape(-1, 2, tokens, head), fresh_at).reshape(-1, 4, 2, tokens, head)
    keys_in = deliver(keys.reshape(-1, hist_rows, head), cached_at).reshape(-1, hist_rows, head)
    values_in = deliver(values.reshape(-1, hist_rows, head), cached_at).reshape(-1, hist_rows, head)

    all_sessions = jnp.arange(64 * sessions, dtype=jnp.int32)
    owned = new_owner[:, 0] == me
    place = jnp.cumsum(owned.astype(jnp.int32)) - 1
    is_slot = jnp.logical_and(owned[None, :], place[None, :] == order[:, None])

    def of_slot(per_session):
        return jnp.sum(jnp.where(is_slot, per_session[None, :], 0), axis=1)

    slot_session = of_slot(all_sessions)
    slot_hist, slot_new = of_slot(history_len), of_slot(new_len)
    holder = slot_session // sessions
    before = jnp.concatenate([jnp.full((1,), -1, jnp.int32), holder[:-1]])
    slot_rank = (holder == before).astype(jnp.int32)
    replicas = jnp.arange(64, dtype=jnp.int32)
    ingest_at = spread_index(replicas)
    holder_hit = ingest_source[None, :] == holder[:, None]
    ingester = jnp.sum(jnp.where(holder_hit, ingest_at[None, :], 0), axis=1)
    slot_from = (ingester % 32) * (2 * CAP) + (ingester // 32) * CAP + slot_rank

    own_source = ingest_source[me]
    own_hist = lax.dynamic_slice(history_len, (own_source * sessions,), (sessions,))
    own_new = lax.dynamic_slice(new_len, (own_source * sessions,), (sessions,))
    attended = attend(new_queries, keys, values, fresh_all, norm_gains, own_hist, own_new, half, shard)
    migrated = build(keys_in, values_in, fresh_in, slot_from, slot_hist, slot_new)
    return attended, migrated


def solution(mesh):
    split = Mesh(mesh.devices.reshape(4, 2, 4, 2, 4), ("x", "zh", "y", "core", "zl"))
    in_specs = (
        P(REPLICA, None, None, "zl"),
        P(REPLICA, "zl", None),
        P(REPLICA, "zl", None, None, None),
        P(),
        P(),
        P(),
        P(),
        P(),
    )
    out_specs = (P(REPLICA, "zl", None), P(REPLICA, None, None, "zl"))
    return jax.shard_map(on_device, mesh=split, in_specs=in_specs, out_specs=out_specs, check_vma=False)
```

```python
import functools

import jax
import jax.numpy as jnp
from jax import lax
from jax.experimental.layout import Layout, with_layout_constraint
from jax.experimental import pallas as pl
from jax.experimental.pallas import tpu as pltpu
from jax.sharding import Mesh, PartitionSpec as P

REPLICA = ("x", "zh", "y", "core")
SPREAD = ("zh", "x", "y", "core")
COLUMN = ("x", "y", "core")
RING = ("zh", "zl")
CAP = 2
EPS = 1e-06
BF16 = jnp.bfloat16
F32 = jnp.float32


def spread_index(replica):
    x, zh, y, core = replica // 16, (replica // 8) % 2, (replica // 2) % 4, replica % 2
    return zh * 32 + x * 8 + y * 2 + core


def replica_at(spread):
    zh, x, y, core = spread // 32, (spread // 8) % 4, (spread // 2) % 4, spread % 2
    return x * 16 + zh * 8 + y * 2 + core


def fresh_rows(ref, index, part):
    shards = ref.shape[1]
    pieces = [ref[(0, i) + index + (part,)].astype(F32) for i in range(shards)]
    return jnp.concatenate(pieces, axis=0).astype(BF16)


def lanes_of(h, groups, head):
    return [slice((h * groups + g) * head, (h * groups + g + 1) * head) for g in range(groups)]


def weigh_kernel(meta, hist_len, q_ref, k_ref, kv_ref, gain_ref, out_ref):
    halves, blocks = pl.program_id(0), pl.program_id(1)
    count, tokens, width = q_ref.shape
    kv_heads, head = k_ref.shape[1], k_ref.shape[5]
    history = k_ref.shape[4]
    groups = width // (kv_heads * head)
    rows = groups * tokens
    fresh = kv_ref.shape[1] * tokens
    keys = out_ref.shape[2]
    first = (halves * pl.num_programs(1) + blocks) * count
    gain = gain_ref[0:1, :].astype(F32)
    scale = head ** (-0.5)
    column = lax.broadcasted_iota(jnp.int32, (kv_heads * rows, keys), 1)
    token = lax.broadcasted_iota(jnp.int32, (kv_heads * rows, keys), 0) % tokens + meta[1] * tokens
    causal = jnp.logical_and(column >= history, column - history <= token)
    padding = jnp.zeros((keys - history - fresh, head), BF16)

    def one_session(s, carry):
        length = jnp.minimum(hist_len[first + s], history)
        allowed = jnp.logical_or(causal, column < length)
        scores = []
        for h in range(kv_heads):
            query = jnp.concatenate([q_ref[s, :, lane].astype(F32) for lane in lanes_of(h, groups, head)], axis=0)
            mean_square = jnp.mean(query * query, axis=-1, keepdims=True)
            query = (query * lax.rsqrt(mean_square + EPS) * gain).astype(BF16)
            key = jnp.concatenate([k_ref[0, h, 0, s], fresh_rows(kv_ref, (h, s), 0), padding], axis=0)
            scores.append(lax.dot_general(query, key, (((1,), (1,)), ((), ())), preferred_element_type=F32))
        scores = jnp.where(allowed, jnp.concatenate(scores, axis=0) * scale, -jnp.inf)
        weight = jnp.exp(scores - jnp.max(scores, axis=-1, keepdims=True))
        out_ref[s] = (weight * (1.0 / jnp.sum(weight, axis=-1, keepdims=True))).astype(BF16)
        return carry

    lax.fori_loop(0, count, one_session, 0, unroll=2)


def mix_kernel(meta, new_len, w_ref, early_ref, late_ref, kv_ref, out_ref):
    halves, blocks = pl.program_id(0), pl.program_id(1)
    count, tokens, width = out_ref.shape
    kv_heads, head = late_ref.shape[1], late_ref.shape[5]
    groups = width // (kv_heads * head)
    rows = groups * tokens
    keys = w_ref.shape[2]
    first = (halves * pl.num_programs(1) + blocks) * count
    used = early_ref.shape[4] + late_ref.shape[4] + kv_ref.shape[1] * tokens
    padding = jnp.zeros((keys - used, head), BF16)
    token = lax.broadcasted_iota(jnp.int32, (rows, head), 0) % tokens + meta[1] * tokens

    def one_session(s, carry):
        live = token < new_len[first + s]
        for h in range(kv_heads):
            pieces = [early_ref[0, h, 0, s], late_ref[0, h, 0, s], fresh_rows(kv_ref, (h, s), 1), padding]
            value = jnp.concatenate(pieces, axis=0)
            mixed = jnp.dot(w_ref[s, h * rows : (h + 1) * rows], value, preferred_element_type=F32)
            mixed = jnp.where(live, mixed, 0.0)
            for g, lane in enumerate(lanes_of(h, groups, head)):
                out_ref[s, :, lane] = mixed[g * tokens : (g + 1) * tokens].astype(BF16)
        return carry

    lax.fori_loop(0, count, one_session, 0, unroll=2)


def cached_spec(part, count, rows, at):
    _, kv_heads, _, _, _, head = part.shape
    return pl.BlockSpec((1, kv_heads, 1, count, rows, head), lambda i, j, m, a: (i, 0, m[0], j, at, 0))


def fresh_spec(fresh, count, blocks):
    _, shards, kv_heads, _, parts, tokens, head = fresh.shape
    return pl.BlockSpec(
        (1, shards, kv_heads, count, parts, tokens, head), lambda i, j, m, a: (m[0], 0, 0, i * blocks + j, 0, 0, 0)
    )


def weigh(queries, early, fresh, gains, hist_len, meta, history):
    sessions, tokens, width = queries.shape
    per_half, _, head = early.shape[3:]
    count = per_half // 2
    blocks = per_half // count
    columns = -(-(history + fresh.shape[1] * tokens) // 128) * 128
    whole = lambda i, j, m, a: (i * blocks + j, 0, 0)
    rows = width // head * tokens
    return pl.pallas_call(
        weigh_kernel,
        out_shape=jax.ShapeDtypeStruct((sessions, rows, columns), BF16),
        grid_spec=pltpu.PrefetchScalarGridSpec(
            num_scalar_prefetch=2,
            grid=(2, blocks),
            in_specs=[
                pl.BlockSpec((count, tokens, width), whole),
                cached_spec(early, count, history, 0),
                fresh_spec(fresh, count, blocks),
                pl.BlockSpec((2, head), lambda i, j, m, a: (0, 0)),
            ],
            out_specs=pl.BlockSpec((count, rows, columns), whole),
        ),
        compiler_params=pltpu.CompilerParams(vmem_limit_bytes=48 * 1024 * 1024),
    )(meta, hist_len, queries, early, fresh, gains)


def mix(weights, early, late, fresh, new_len, meta, width, history):
    sessions = weights.shape[0]
    tokens = fresh.shape[5]
    count = late.shape[3] // 2
    blocks = late.shape[3] // count
    early_rows = early.shape[4] - history
    whole = lambda i, j, m, a: (i * blocks + j, 0, 0)
    return pl.pallas_call(
        mix_kernel,
        out_shape=jax.ShapeDtypeStruct((sessions, tokens, width), BF16),
        grid_spec=pltpu.PrefetchScalarGridSpec(
            num_scalar_prefetch=2,
            grid=(2, blocks),
            in_specs=[
                pl.BlockSpec((count,) + weights.shape[1:], whole),
                cached_spec(early, count, early_rows, history // early_rows),
                cached_spec(late, count, late.shape[4], 0),
                fresh_spec(fresh, count, blocks),
            ],
            out_specs=pl.BlockSpec((count, tokens, width), whole),
        ),
        compiler_params=pltpu.CompilerParams(vmem_limit_bytes=48 * 1024 * 1024),
    )(meta, new_len, weights, early, late, fresh)


def build_kernel(pieces, slot_from, hist_len, new_len, *refs):
    cached_refs, kv_ref, out_ref = refs[:pieces], refs[pieces], refs[-1]
    count, _, rows, head = out_ref.shape
    shards = kv_ref.shape[1]
    tokens = kv_ref.shape[3]
    history = rows - shards * tokens
    target_row = lax.broadcasted_iota(jnp.int32, (rows, rows), 0)
    source = lax.broadcasted_iota(jnp.int32, (rows, rows), 1)

    def one_slot(j, carry):
        at, length, live = slot_from[j], hist_len[j], new_len[j]
        moved = jnp.where(source - history < live, source - history + length, -1)
        target = jnp.where(source < history, jnp.where(source < length, source, -1), moved)
        pick = (target_row == target).astype(F32).astype(BF16)
        fresh = [kv_ref[at, i, 0].astype(F32) for i in range(shards)]
        held = [ref[at] for ref in cached_refs]
        rows_in = jnp.concatenate(held + [jnp.concatenate(fresh, axis=0).astype(BF16)], axis=0)
        out_ref[j, 0] = jnp.dot(pick, rows_in, preferred_element_type=F32).astype(BF16)
        return carry

    lax.fori_loop(0, count, one_slot, 0, unroll=4)


def build(part, pieces, fresh, slot_from, hist_len, new_len, into=None):
    slots, shards, _, tokens, head = fresh.shape
    count = slot_from.shape[0]
    rows = sum(piece[1] for piece in pieces) + shards * tokens
    smem = pl.BlockSpec(memory_space=pltpu.SMEM)
    in_specs = [smem, smem, smem]
    for _, piece_rows, at in pieces:
        in_specs.append(pl.BlockSpec((slots, piece_rows, head), lambda i, at=at: (0, at, 0)))
    in_specs.append(pl.BlockSpec((slots, shards, 1, tokens, head), lambda i: (0, 0, part, 0, 0)))
    operands = [slot_from, hist_len, new_len] + [piece for piece, _, _ in pieces] + [fresh]
    aliases = {}
    if into is not None:
        aliases = {len(in_specs): 0}
        in_specs.append(pl.BlockSpec(memory_space=pl.ANY))
        operands.append(into)
    return pl.pallas_call(
        functools.partial(build_kernel, len(pieces)),
        out_shape=jax.ShapeDtypeStruct((count, 2, rows, head), BF16),
        grid=(1,),
        in_specs=in_specs,
        out_specs=pl.BlockSpec((count, 1, rows, head), lambda i: (0, part, 0, 0)),
        input_output_aliases=aliases,
        compiler_params=pltpu.CompilerParams(vmem_limit_bytes=48 * 1024 * 1024),
    )(*operands)


def on_device(history, new_queries, new_kv, norm_gains, ingest_source, new_owner, history_len, new_len):
    sessions, _, hist_rows, head = history.shape
    half_sessions = sessions // 2
    tokens, kv_heads = new_kv.shape[1], new_kv.shape[2]
    half, shard = lax.axis_index("zh"), lax.axis_index("zl")
    me = lax.axis_index(REPLICA)
    column = lax.axis_index(COLUMN)

    raw_key = new_kv[:, :, :, 0, :].astype(F32)
    mean_square = jnp.mean(raw_key * raw_key, axis=-1, keepdims=True)
    normed = (raw_key * lax.rsqrt(mean_square + EPS) * norm_gains[1].astype(F32)).astype(BF16)
    fresh = jnp.stack([normed, new_kv[:, :, :, 1, :]], axis=0).transpose(3, 1, 0, 2, 4)
    fresh = with_layout_constraint(fresh, Layout(major_to_minor=(0, 1, 2, 3, 4)))

    source_spread = spread_index(ingest_source[replica_at(jnp.arange(64, dtype=jnp.int32))])
    source_order = source_spread.reshape(2, 32).T.reshape(64)

    def spread(part):
        return lax.all_to_all(part.reshape(64, -1, head), SPREAD, split_axis=0, concat_axis=0, tiled=True)

    def gather(pieces):
        picked = jnp.take(pieces, source_order, axis=0, mode="clip").reshape(32, 2, -1, head)
        held = lax.all_to_all(picked, COLUMN, split_axis=0, concat_axis=1)
        return held.reshape(2, half_sessions, -1, head)

    tie = lax.optimization_barrier
    late_rows = hist_rows // 2
    early_rows = hist_rows - late_rows
    both = history.reshape(sessions, 2 * hist_rows, head)
    early_part, late_part, fresh = tie((both[:, :-late_rows], both[:, -late_rows:], fresh))
    early_spread = spread(early_part)
    late_part, early_spread = tie((late_part, early_spread))
    late_spread = spread(late_part)
    early_held = gather(early_spread)
    late_spread, early_held = tie((late_spread, early_held))
    late_held = gather(late_spread)

    fresh_all = lax.all_gather(fresh, RING, axis=0).reshape((2, 4) + fresh.shape)
    early = lax.all_gather(early_held, RING, axis=0).reshape((2, 4) + early_held.shape)
    late = lax.all_gather(late_held, RING, axis=0).reshape((2, 4) + late_held.shape)

    owners = new_owner[:, 0].reshape(64, sessions)
    mine = ingest_source[replica_at(jnp.arange(2, dtype=jnp.int32) * 32 + column)]
    mine_owner = owners[mine]
    order = jnp.arange(sessions, dtype=jnp.int32)
    same = mine_owner[:, :, None] == mine_owner[:, None, :]
    rank = jnp.sum(jnp.logical_and(same, order[None, None, :] < order[None, :, None]), axis=2)
    target = replica_at(half * 32 + jnp.arange(32, dtype=jnp.int32))
    hit = jnp.logical_and(
        mine_owner[None, :, None, :] == target[:, None, None, None],
        rank[None, :, None, :] == jnp.arange(CAP)[None, None, :, None],
    )
    chosen = jnp.sum(jnp.where(hit, order, 0), axis=3).reshape(32, 2 * CAP)
    from_half = (jnp.arange(2 * CAP, dtype=jnp.int32) // CAP)[None, :]
    block = ((chosen // half_sessions) * 4 + shard) * 2 + from_half
    cached_at = (block * half_sessions + chosen % half_sessions).reshape(-1)
    fresh_at = (from_half * 4)[:, :, None] + jnp.arange(4, dtype=jnp.int32)
    fresh_at = ((fresh_at * kv_heads + shard) * sessions + chosen[:, :, None]).reshape(-1)

    def deliver(rows, at):
        sent = jnp.take(rows, at, axis=0, mode="clip").reshape((32, -1) + rows.shape[1:])
        return lax.all_to_all(sent, COLUMN, split_axis=0, concat_axis=0, tiled=True)

    fresh_in = deliver(fresh_all.reshape(-1, 2, tokens, head), fresh_at).reshape(-1, 4, 2, tokens, head)
    def deliver_cached(part):
        rows = part.shape[4]
        return deliver(part.reshape(-1, rows, head), cached_at).reshape(-1, rows, head)

    all_sessions = jnp.arange(64 * sessions, dtype=jnp.int32)
    owned = new_owner[:, 0] == me
    place = jnp.cumsum(owned.astype(jnp.int32)) - 1
    is_slot = jnp.logical_and(owned[None, :], place[None, :] == order[:, None])

    def of_slot(per_session):
        return jnp.sum(jnp.where(is_slot, per_session[None, :], 0), axis=1)

    slot_session = of_slot(all_sessions)
    slot_hist, slot_new = of_slot(history_len), of_slot(new_len)
    holder = slot_session // sessions
    before = jnp.concatenate([jnp.full((1,), -1, jnp.int32), holder[:-1]])
    slot_rank = (holder == before).astype(jnp.int32)
    replicas = jnp.arange(64, dtype=jnp.int32)
    ingest_at = spread_index(replicas)
    holder_hit = ingest_source[None, :] == holder[:, None]
    ingester = jnp.sum(jnp.where(holder_hit, ingest_at[None, :], 0), axis=1)
    slot_from = (ingester % 32) * (2 * CAP) + (ingester // 32) * CAP + slot_rank

    own_source = ingest_source[me]
    own_hist = lax.dynamic_slice(history_len, (own_source * sessions,), (sessions,))
    own_new = lax.dynamic_slice(new_len, (own_source * sessions,), (sessions,))
    meta = jnp.stack([half, shard]).astype(jnp.int32)
    slots = (slot_from, slot_hist, slot_new)
    early, fresh_in = tie((early, fresh_in))
    early_in = deliver_cached(early)
    weights = weigh(new_queries, early, fresh_all, norm_gains, own_hist, meta, hist_rows)
    migrated = build(0, [(early_in, hist_rows, 0)], fresh_in, *slots)
    late, weights = tie((late, weights))
    late_in = deliver_cached(late)
    attended = mix(weights, early, late, fresh_all, own_new, meta, new_queries.shape[2], hist_rows)
    value_pieces = [(early_in, early_rows, hist_rows // early_rows), (late_in, late_rows, 0)]
    migrated = build(1, value_pieces, fresh_in, *slots, into=migrated)
    return attended, migrated


def solution(mesh):
    split = Mesh(mesh.devices.reshape(4, 2, 4, 2, 4), ("x", "zh", "y", "core", "zl"))
    in_specs = (
        P(REPLICA, None, None, "zl"),
        P(REPLICA, "zl", None),
        P(REPLICA, "zl", None, None, None),
        P(),
        P(),
        P(),
        P(),
        P(),
    )
    out_specs = (P(REPLICA, "zl", None), P(REPLICA, None, None, "zl"))
    return jax.shard_map(on_device, mesh=split, in_specs=in_specs, out_specs=out_specs, check_vma=False)
```

```python
import functools

import jax
import jax.numpy as jnp
from jax import lax
from jax.experimental.layout import Layout, with_layout_constraint
from jax.experimental import pallas as pl
from jax.experimental.pallas import tpu as pltpu
from jax.sharding import Mesh, PartitionSpec as P

REPLICA = ("x", "zh", "y", "core")
SPREAD = ("zh", "x", "y", "core")
COLUMN = ("x", "y", "core")
RING = ("zh", "zl")
CAP = 2
SHARDS = 4
UNIT = 16
UNITS = 4
KEPT = 24
EPS = 1e-06
BF16 = jnp.bfloat16
F32 = jnp.float32


def spread_index(replica):
    x, zh, y, core = replica // 16, (replica // 8) % 2, (replica // 2) % 4, replica % 2
    return zh * 32 + x * 8 + y * 2 + core


def replica_at(spread):
    zh, x, y, core = spread // 32, (spread // 8) % 4, (spread // 2) % 4, spread % 2
    return x * 16 + zh * 8 + y * 2 + core


def fresh_rows(ref, index, part):
    shards = ref.shape[1]
    pieces = [ref[(0, i) + index + (part,)].astype(F32) for i in range(shards)]
    return jnp.concatenate(pieces, axis=0).astype(BF16)


def lanes_of(h, groups, head):
    return [slice((h * groups + g) * head, (h * groups + g + 1) * head) for g in range(groups)]


def unit_place(ref, first, step):
    per_half = ref.shape[3]
    at = jnp.minimum(first + step, 2 * per_half - 1)
    upper = (at >= per_half).astype(jnp.int32)
    return upper, at - upper * per_half


def weigh_kernel(meta, hist_len, unit_first, q_ref, early_ref, kv_ref, gain_ref, out_ref):
    count, tokens, width = q_ref.shape
    kv_heads, head = early_ref.shape[1], early_ref.shape[5]
    groups = width // (kv_heads * head)
    rows = groups * tokens
    fresh = kv_ref.shape[1] * tokens
    keys = out_ref.shape[2]
    history = UNITS * UNIT
    first = pl.program_id(0) * count
    gain = gain_ref[0:1, :].astype(F32)
    scale = head ** (-0.5)
    column = lax.broadcasted_iota(jnp.int32, (kv_heads * rows, keys), 1)
    token = lax.broadcasted_iota(jnp.int32, (kv_heads * rows, keys), 0) % tokens + meta[1] * tokens
    causal = jnp.logical_and(column >= history, column - history <= token)
    padding = jnp.zeros((keys - history - fresh, head), BF16)

    def one_session(s, carry):
        length = jnp.minimum(hist_len[first + s], history)
        allowed = jnp.logical_or(causal, column < length)
        places = [unit_place(early_ref, unit_first[first + s], q) for q in range(UNITS)]
        scores = []
        for h in range(kv_heads):
            query = jnp.concatenate([q_ref[s, :, lane].astype(F32) for lane in lanes_of(h, groups, head)], axis=0)
            mean_square = jnp.mean(query * query, axis=-1, keepdims=True)
            query = (query * lax.rsqrt(mean_square + EPS) * gain).astype(BF16)
            cached = [early_ref[upper, h, 0, at, 0:UNIT, :] for upper, at in places]
            key = jnp.concatenate(cached + [fresh_rows(kv_ref, (h, s), 0), padding], axis=0)
            scores.append(lax.dot_general(query, key, (((1,), (1,)), ((), ())), preferred_element_type=F32))
        scores = jnp.where(allowed, jnp.concatenate(scores, axis=0) * scale, -jnp.inf)
        weight = jnp.exp(scores - jnp.max(scores, axis=-1, keepdims=True))
        out_ref[s] = (weight * (1.0 / jnp.sum(weight, axis=-1, keepdims=True))).astype(BF16)
        return carry

    lax.fori_loop(0, count, one_session, 0, unroll=2)


def mix_kernel(meta, new_len, unit_first, w_ref, early_ref, late_ref, kv_ref, out_ref):
    count, tokens, width = out_ref.shape
    kv_heads, head = late_ref.shape[1], late_ref.shape[5]
    groups = width // (kv_heads * head)
    rows = groups * tokens
    keys = w_ref.shape[2]
    first = pl.program_id(0) * count
    fresh = kv_ref.shape[1] * tokens
    padding = jnp.zeros((keys - UNITS * UNIT - fresh, head), BF16)
    token = lax.broadcasted_iota(jnp.int32, (rows, head), 0) % tokens + meta[1] * tokens

    def one_session(s, carry):
        live = token < new_len[first + s]
        places = [unit_place(late_ref, unit_first[first + s], q) for q in range(UNITS)]
        for h in range(kv_heads):
            cached = []
            for upper, at in places:
                cached.append(early_ref[upper, h, 0, at, UNIT:KEPT, :].astype(F32))
                cached.append(late_ref[upper, h, 0, at].astype(F32))
            cached = jnp.concatenate(cached, axis=0).astype(BF16)
            value = jnp.concatenate([cached, fresh_rows(kv_ref, (h, s), 1), padding], axis=0)
            mixed = jnp.dot(w_ref[s, h * rows : (h + 1) * rows], value, preferred_element_type=F32)
            mixed = jnp.where(live, mixed, 0.0)
            for g, lane in enumerate(lanes_of(h, groups, head)):
                out_ref[s, :, lane] = mixed[g * tokens : (g + 1) * tokens].astype(BF16)
        return carry

    lax.fori_loop(0, count, one_session, 0, unroll=2)


def units_spec(part):
    halves, kv_heads, _, per_half, rows, head = part.shape
    return pl.BlockSpec((halves, kv_heads, 1, per_half, rows, head), lambda i, m, a, b: (0, 0, m[0], 0, 0, 0))


def fresh_spec(fresh, count):
    _, shards, kv_heads, _, parts, tokens, head = fresh.shape
    return pl.BlockSpec((1, shards, kv_heads, count, parts, tokens, head), lambda i, m, a, b: (m[0], 0, 0, i, 0, 0, 0))


def weigh(queries, early, fresh, gains, hist_len, unit_first, meta):
    sessions, tokens, width = queries.shape
    head = early.shape[5]
    count = sessions // 4
    columns = -(-(UNITS * UNIT + fresh.shape[1] * tokens) // 128) * 128
    whole = lambda i, m, a, b: (i, 0, 0)
    rows = width // head * tokens
    return pl.pallas_call(
        weigh_kernel,
        out_shape=jax.ShapeDtypeStruct((sessions, rows, columns), BF16),
        grid_spec=pltpu.PrefetchScalarGridSpec(
            num_scalar_prefetch=3,
            grid=(sessions // count,),
            in_specs=[
                pl.BlockSpec((count, tokens, width), whole),
                units_spec(early),
                fresh_spec(fresh, count),
                pl.BlockSpec((2, head), lambda i, m, a, b: (0, 0)),
            ],
            out_specs=pl.BlockSpec((count, rows, columns), whole),
        ),
        compiler_params=pltpu.CompilerParams(vmem_limit_bytes=48 * 1024 * 1024),
    )(meta, hist_len, unit_first, queries, early, fresh, gains)


def mix(weights, early, late, fresh, new_len, unit_first, meta, width):
    sessions = weights.shape[0]
    tokens = fresh.shape[5]
    count = sessions // 4
    whole = lambda i, m, a, b: (i, 0, 0)
    return pl.pallas_call(
        mix_kernel,
        out_shape=jax.ShapeDtypeStruct((sessions, tokens, width), BF16),
        grid_spec=pltpu.PrefetchScalarGridSpec(
            num_scalar_prefetch=3,
            grid=(sessions // count,),
            in_specs=[
                pl.BlockSpec((count,) + weights.shape[1:], whole),
                units_spec(early),
                units_spec(late),
                fresh_spec(fresh, count),
            ],
            out_specs=pl.BlockSpec((count, tokens, width), whole),
        ),
        compiler_params=pltpu.CompilerParams(vmem_limit_bytes=48 * 1024 * 1024),
    )(meta, new_len, unit_first, weights, early, late, fresh)


def build_kernel(part, slot_from, hist_len, new_len, *refs):
    cached_refs, kv_ref, out_ref = refs[: part + 1], refs[part + 1], refs[-1]
    count, _, rows, head = out_ref.shape
    shards = kv_ref.shape[1]
    tokens = kv_ref.shape[3]
    history = rows - shards * tokens
    target_row = lax.broadcasted_iota(jnp.int32, (rows, rows), 0)
    source = lax.broadcasted_iota(jnp.int32, (rows, rows), 1)

    def one_slot(j, carry):
        at, length, live = slot_from[j], hist_len[j], new_len[j]
        moved = jnp.where(source - history < live, source - history + length, -1)
        target = jnp.where(source < history, jnp.where(source < length, source, -1), moved)
        pick = (target_row == target).astype(F32).astype(BF16)
        rows_in = []
        for q in range(UNITS):
            if part == 0:
                rows_in.append(cached_refs[0][at, q, 0:UNIT, :].astype(F32))
            else:
                rows_in.append(cached_refs[0][at, q, UNIT:KEPT, :].astype(F32))
                rows_in.append(cached_refs[1][at, q].astype(F32))
        rows_in += [kv_ref[at, i, 0].astype(F32) for i in range(shards)]
        rows_in = jnp.concatenate(rows_in, axis=0).astype(BF16)
        out_ref[j, 0] = jnp.dot(pick, rows_in, preferred_element_type=F32).astype(BF16)
        return carry

    lax.fori_loop(0, count, one_slot, 0, unroll=4)


def build(part, pieces, fresh, slot_from, hist_len, new_len, into=None):
    slots, shards, _, tokens, head = fresh.shape
    count = slot_from.shape[0]
    rows = UNITS * UNIT + shards * tokens
    smem = pl.BlockSpec(memory_space=pltpu.SMEM)
    in_specs = [smem, smem, smem]
    for piece in pieces:
        in_specs.append(pl.BlockSpec(piece.shape, lambda i: (0, 0, 0, 0)))
    in_specs.append(pl.BlockSpec((slots, shards, 1, tokens, head), lambda i: (0, 0, part, 0, 0)))
    operands = [slot_from, hist_len, new_len, *pieces, fresh]
    aliases = {}
    if into is not None:
        aliases = {len(in_specs): 0}
        in_specs.append(pl.BlockSpec(memory_space=pl.ANY))
        operands.append(into)
    return pl.pallas_call(
        functools.partial(build_kernel, part),
        out_shape=jax.ShapeDtypeStruct((count, 2, rows, head), BF16),
        grid=(1,),
        in_specs=in_specs,
        out_specs=pl.BlockSpec((count, 1, rows, head), lambda i: (0, part, 0, 0)),
        input_output_aliases=aliases,
        compiler_params=pltpu.CompilerParams(vmem_limit_bytes=48 * 1024 * 1024),
    )(*operands)


def units_of(lengths):
    return (lengths + UNIT - 1) // UNIT


def run(capacity, history, new_queries, new_kv, norm_gains, ingest_source, new_owner, history_len, new_len):
    sessions, _, hist_rows, head = history.shape
    per_half = capacity // 2
    tokens, kv_heads = new_kv.shape[1], new_kv.shape[2]
    half, shard = lax.axis_index("zh"), lax.axis_index("zl")
    me = lax.axis_index(REPLICA)
    column = lax.axis_index(COLUMN)
    tie = lax.optimization_barrier
    lengths = history_len.reshape(64, sessions)

    raw_key = new_kv[:, :, :, 0, :].astype(F32)
    mean_square = jnp.mean(raw_key * raw_key, axis=-1, keepdims=True)
    normed = (raw_key * lax.rsqrt(mean_square + EPS) * norm_gains[1].astype(F32)).astype(BF16)
    fresh = jnp.stack([normed, new_kv[:, :, :, 1, :]], axis=0).transpose(3, 1, 0, 2, 4)
    fresh = with_layout_constraint(fresh, Layout(major_to_minor=(0, 1, 2, 3, 4)))

    held_units = units_of(lax.dynamic_slice(history_len, (me * sessions,), (sessions,)))
    slot = jnp.arange(capacity, dtype=jnp.int32)
    passed = jnp.cumsum(held_units)[None, :] <= slot[:, None]
    unit_session = jnp.minimum(jnp.sum(passed.astype(jnp.int32), axis=1), sessions - 1)
    unit_step = jnp.clip(slot - jnp.sum(jnp.where(passed, held_units[None, :], 0), axis=1), 0, UNITS - 1)
    key_unit = unit_session * (2 * UNITS) + unit_step
    fresh, key_unit = tie((fresh, key_unit))
    fresh_all = lax.all_gather(fresh, RING, axis=0).reshape((2, SHARDS) + fresh.shape)
    cached = history.reshape(-1, UNIT, head)
    packed_keys = jnp.take(cached, key_unit, axis=0, mode="clip")
    packed_values = jnp.take(cached, key_unit + UNITS, axis=0, mode="clip")

    source_spread = spread_index(ingest_source[replica_at(jnp.arange(64, dtype=jnp.int32))])
    source_order = source_spread.reshape(2, 32).T.reshape(64)

    def spread(part):
        return lax.all_to_all(part.reshape(64, -1, head), SPREAD, split_axis=0, concat_axis=0, tiled=True)

    def gather(pieces, rows):
        picked = jnp.take(pieces, source_order, axis=0, mode="clip").reshape(32, 2, -1, head)
        held = lax.all_to_all(picked, COLUMN, split_axis=0, concat_axis=1)
        return held.reshape(2, per_half, rows, head)

    early_part = jnp.concatenate([packed_keys, packed_values[:, : KEPT - UNIT]], axis=1)
    late_part = packed_values[:, KEPT - UNIT :]
    early_spread = spread(early_part)
    late_part, early_spread = tie((late_part, early_spread))
    late_spread = spread(late_part)
    early_held = gather(early_spread, KEPT)
    late_spread, early_held = tie((late_spread, early_held))
    late_held = gather(late_spread, 2 * UNIT - KEPT)
    early = lax.all_gather(early_held, RING, axis=0).reshape((2, SHARDS) + early_held.shape)
    late = lax.all_gather(late_held, RING, axis=0).reshape((2, SHARDS) + late_held.shape)

    owners = new_owner[:, 0].reshape(64, sessions)
    mine = ingest_source[replica_at(jnp.arange(2, dtype=jnp.int32) * 32 + column)]
    mine_owner = owners[mine]
    order = jnp.arange(sessions, dtype=jnp.int32)
    same = mine_owner[:, :, None] == mine_owner[:, None, :]
    rank = jnp.sum(jnp.logical_and(same, order[None, None, :] < order[None, :, None]), axis=2)
    target = replica_at(half * 32 + jnp.arange(32, dtype=jnp.int32))
    hit = jnp.logical_and(
        mine_owner[None, :, None, :] == target[:, None, None, None],
        rank[None, :, None, :] == jnp.arange(CAP)[None, None, :, None],
    )
    mine_units = units_of(lengths[mine])
    mine_first = jnp.cumsum(mine_units, axis=1) - mine_units
    chosen = jnp.sum(jnp.where(hit, order, 0), axis=3).reshape(32, 2 * CAP)
    chosen_first = jnp.sum(jnp.where(hit, mine_first[None, :, None, :], 0), axis=3).reshape(32, 2 * CAP)
    from_half = (jnp.arange(2 * CAP, dtype=jnp.int32) // CAP)[None, :]
    unit = jnp.minimum(chosen_first[:, :, None] + jnp.arange(UNITS, dtype=jnp.int32), capacity - 1)
    block = ((unit // per_half) * SHARDS + shard) * 2 + from_half[:, :, None]
    cached_at = (block * per_half + unit % per_half).reshape(-1)
    fresh_at = (from_half * SHARDS)[:, :, None] + jnp.arange(SHARDS, dtype=jnp.int32)
    fresh_at = ((fresh_at * kv_heads + shard) * sessions + chosen[:, :, None]).reshape(-1)

    def deliver(rows, at):
        sent = jnp.take(rows, at, axis=0, mode="clip").reshape((32, -1) + rows.shape[1:])
        return lax.all_to_all(sent, COLUMN, split_axis=0, concat_axis=0, tiled=True)

    fresh_in = deliver(fresh_all.reshape(-1, 2, tokens, head), fresh_at).reshape(-1, SHARDS, 2, tokens, head)

    def deliver_cached(part):
        rows = part.shape[4]
        return deliver(part.reshape(-1, rows, head), cached_at).reshape(-1, UNITS, rows, head)

    all_sessions = jnp.arange(64 * sessions, dtype=jnp.int32)
    owned = new_owner[:, 0] == me
    place = jnp.cumsum(owned.astype(jnp.int32)) - 1
    is_slot = jnp.logical_and(owned[None, :], place[None, :] == order[:, None])

    def of_slot(per_session):
        return jnp.sum(jnp.where(is_slot, per_session[None, :], 0), axis=1)

    slot_session = of_slot(all_sessions)
    slot_hist, slot_new = of_slot(history_len), of_slot(new_len)
    holder = slot_session // sessions
    before = jnp.concatenate([jnp.full((1,), -1, jnp.int32), holder[:-1]])
    slot_rank = (holder == before).astype(jnp.int32)
    replicas = jnp.arange(64, dtype=jnp.int32)
    ingest_at = spread_index(replicas)
    holder_hit = ingest_source[None, :] == holder[:, None]
    ingester = jnp.sum(jnp.where(holder_hit, ingest_at[None, :], 0), axis=1)
    slot_from = (ingester % 32) * (2 * CAP) + (ingester // 32) * CAP + slot_rank

    own_source = ingest_source[me]
    own_hist = lax.dynamic_slice(history_len, (own_source * sessions,), (sessions,))
    own_new = lax.dynamic_slice(new_len, (own_source * sessions,), (sessions,))
    own_first = jnp.cumsum(units_of(own_hist)) - units_of(own_hist)
    meta = jnp.stack([half, shard]).astype(jnp.int32)
    slots = (slot_from, slot_hist, slot_new)
    early, fresh_in = tie((early, fresh_in))
    early_in = deliver_cached(early)
    weights = weigh(new_queries, early, fresh_all, norm_gains, own_hist, own_first, meta)
    migrated = build(0, [early_in], fresh_in, *slots)
    late, weights = tie((late, weights))
    late_in = deliver_cached(late)
    attended = mix(weights, early, late, fresh_all, own_new, own_first, meta, new_queries.shape[2])
    migrated = build(1, [early_in, late_in], fresh_in, *slots, into=migrated)
    return attended, migrated


def on_device(*arrays):
    history_len = arrays[6]
    sessions = arrays[0].shape[0]
    whole = sessions * UNITS
    short = whole * 11 // 14
    most = jnp.max(jnp.sum(units_of(history_len).reshape(64, sessions), axis=1))
    return lax.cond(most <= short, functools.partial(run, short), functools.partial(run, whole), *arrays)


def solution(mesh):
    split = Mesh(mesh.devices.reshape(4, 2, 4, 2, 4), ("x", "zh", "y", "core", "zl"))
    in_specs = (
        P(REPLICA, None, None, "zl"),
        P(REPLICA, "zl", None),
        P(REPLICA, "zl", None, None, None),
        P(),
        P(),
        P(),
        P(),
        P(),
    )
    out_specs = (P(REPLICA, "zl", None), P(REPLICA, None, None, "zl"))
    return jax.shard_map(on_device, mesh=split, in_specs=in_specs, out_specs=out_specs, check_vma=False)
```

```python
import functools

import jax
import jax.numpy as jnp
from jax import lax
from jax.experimental.layout import Layout, with_layout_constraint
from jax.experimental import pallas as pl
from jax.experimental.pallas import tpu as pltpu
from jax.sharding import Mesh, PartitionSpec as P

REPLICA = ("x", "zh", "y", "core")
SPREAD = ("zh", "x", "y", "core")
COLUMN = ("x", "y", "core")
RING = ("zh", "zl")
CAP = 2
SHARDS = 4
UNIT = 16
UNITS = 4
KEPT = 24
EPS = 1e-06
BF16 = jnp.bfloat16
F32 = jnp.float32


def spread_index(replica):
    x, zh, y, core = replica // 16, (replica // 8) % 2, (replica // 2) % 4, replica % 2
    return zh * 32 + x * 8 + y * 2 + core


def replica_at(spread):
    zh, x, y, core = spread // 32, (spread // 8) % 4, (spread // 2) % 4, spread % 2
    return x * 16 + zh * 8 + y * 2 + core


def fresh_rows(ref, index):
    shards = ref.shape[1]
    pieces = [ref[(0, i) + index + (0,)].astype(F32) for i in range(shards)]
    return jnp.concatenate(pieces, axis=0).astype(BF16)


def lanes_of(h, groups, head):
    return [slice((h * groups + g) * head, (h * groups + g + 1) * head) for g in range(groups)]


def unit_place(ref, first, step):
    per_half = ref.shape[3]
    at = jnp.minimum(first + step, 2 * per_half - 1)
    upper = (at >= per_half).astype(jnp.int32)
    return upper, at - upper * per_half


def weigh_kernel(meta, hist_len, unit_first, q_ref, early_ref, kv_ref, gain_ref, out_ref):
    count, tokens, width = q_ref.shape
    kv_heads, head = early_ref.shape[1], early_ref.shape[5]
    groups = width // (kv_heads * head)
    rows = groups * tokens
    fresh = kv_ref.shape[1] * tokens
    keys = out_ref.shape[2]
    history = UNITS * UNIT
    first = pl.program_id(0) * count
    gain = gain_ref[0:1, :].astype(F32)
    scale = head ** (-0.5)
    column = lax.broadcasted_iota(jnp.int32, (kv_heads * rows, keys), 1)
    token = lax.broadcasted_iota(jnp.int32, (kv_heads * rows, keys), 0) % tokens + meta[1] * tokens
    causal = jnp.logical_and(column >= history, column - history <= token)
    padding = jnp.zeros((keys - history - fresh, head), BF16)

    def one_session(s, carry):
        length = jnp.minimum(hist_len[first + s], history)
        allowed = jnp.logical_or(causal, column < length)
        places = [unit_place(early_ref, unit_first[first + s], q) for q in range(UNITS)]
        scores = []
        for h in range(kv_heads):
            query = jnp.concatenate([q_ref[s, :, lane].astype(F32) for lane in lanes_of(h, groups, head)], axis=0)
            mean_square = jnp.mean(query * query, axis=-1, keepdims=True)
            query = (query * lax.rsqrt(mean_square + EPS) * gain).astype(BF16)
            cached = [early_ref[upper, h, 0, at] for upper, at in places]
            key = jnp.concatenate(cached + [fresh_rows(kv_ref, (h, s)), padding], axis=0)
            scores.append(lax.dot_general(query, key, (((1,), (1,)), ((), ())), preferred_element_type=F32))
        scores = jnp.where(allowed, jnp.concatenate(scores, axis=0) * scale, -jnp.inf)
        weight = jnp.exp(scores - jnp.max(scores, axis=-1, keepdims=True))
        out_ref[s] = (weight * (1.0 / jnp.sum(weight, axis=-1, keepdims=True))).astype(BF16)
        return carry

    lax.fori_loop(0, count, one_session, 0, unroll=2)


def mix_kernel(meta, new_len, unit_first, w_ref, early_ref, late_ref, kv_ref, out_ref):
    count, tokens, width = out_ref.shape
    kv_heads, head = late_ref.shape[1], late_ref.shape[5]
    groups = width // (kv_heads * head)
    rows = groups * tokens
    keys = w_ref.shape[2]
    first = pl.program_id(0) * count
    fresh = kv_ref.shape[1] * tokens
    padding = jnp.zeros((keys - UNITS * UNIT - fresh, head), BF16)
    token = lax.broadcasted_iota(jnp.int32, (rows, head), 0) % tokens + meta[1] * tokens

    def one_session(s, carry):
        live = token < new_len[first + s]
        places = [unit_place(late_ref, unit_first[first + s], q) for q in range(UNITS)]
        for h in range(kv_heads):
            cached = []
            for upper, at in places:
                cached.append(early_ref[upper, h, 0, at].astype(F32)[UNIT:])
                cached.append(late_ref[upper, h, 0, at].astype(F32))
            cached = jnp.concatenate(cached, axis=0).astype(BF16)
            value = jnp.concatenate([cached, fresh_rows(kv_ref, (h, s)), padding], axis=0)
            mixed = jnp.dot(w_ref[s, h * rows : (h + 1) * rows], value, preferred_element_type=F32)
            mixed = jnp.where(live, mixed, 0.0)
            for g, lane in enumerate(lanes_of(h, groups, head)):
                out_ref[s, :, lane] = mixed[g * tokens : (g + 1) * tokens].astype(BF16)
        return carry

    lax.fori_loop(0, count, one_session, 0, unroll=2)


def units_spec(part, rows, at):
    halves, kv_heads, _, per_half, _, head = part.shape
    return pl.BlockSpec((halves, kv_heads, 1, per_half, rows, head), lambda i, m, a, b: (0, 0, m[0], 0, at, 0))


def fresh_spec(fresh, count, part):
    _, shards, kv_heads, _, _, tokens, head = fresh.shape
    return pl.BlockSpec((1, shards, kv_heads, count, 1, tokens, head), lambda i, m, a, b: (m[0], 0, 0, i, part, 0, 0))


def weigh(queries, early, fresh, gains, hist_len, unit_first, meta):
    sessions, tokens, width = queries.shape
    head = early.shape[5]
    count = sessions // 4
    columns = -(-(UNITS * UNIT + fresh.shape[1] * tokens) // 128) * 128
    whole = lambda i, m, a, b: (i, 0, 0)
    rows = width // head * tokens
    return pl.pallas_call(
        weigh_kernel,
        out_shape=jax.ShapeDtypeStruct((sessions, rows, columns), BF16),
        grid_spec=pltpu.PrefetchScalarGridSpec(
            num_scalar_prefetch=3,
            grid=(sessions // count,),
            in_specs=[
                pl.BlockSpec((count, tokens, width), whole),
                units_spec(early, UNIT, 0),
                fresh_spec(fresh, count, 0),
                pl.BlockSpec((2, head), lambda i, m, a, b: (0, 0)),
            ],
            out_specs=pl.BlockSpec((count, rows, columns), whole),
        ),
        compiler_params=pltpu.CompilerParams(vmem_limit_bytes=48 * 1024 * 1024),
    )(meta, hist_len, unit_first, queries, early, fresh, gains)


def mix(weights, early, late, fresh, new_len, unit_first, meta, width):
    sessions = weights.shape[0]
    tokens = fresh.shape[5]
    count = sessions // 4
    whole = lambda i, m, a, b: (i, 0, 0)
    return pl.pallas_call(
        mix_kernel,
        out_shape=jax.ShapeDtypeStruct((sessions, tokens, width), BF16),
        grid_spec=pltpu.PrefetchScalarGridSpec(
            num_scalar_prefetch=3,
            grid=(sessions // count,),
            in_specs=[
                pl.BlockSpec((count,) + weights.shape[1:], whole),
                units_spec(early, KEPT, 0),
                units_spec(late, late.shape[4], 0),
                fresh_spec(fresh, count, 1),
            ],
            out_specs=pl.BlockSpec((count, tokens, width), whole),
        ),
        compiler_params=pltpu.CompilerParams(vmem_limit_bytes=48 * 1024 * 1024),
    )(meta, new_len, unit_first, weights, early, late, fresh)


def build_kernel(slot_from, hist_len, new_len, early_ref, late_ref, kv_ref, out_ref):
    count, _, rows, head = out_ref.shape
    shards = kv_ref.shape[1]
    tokens = kv_ref.shape[3]
    history = rows - shards * tokens
    first = pl.program_id(0) * count
    target_row = lax.broadcasted_iota(jnp.int32, (rows, rows), 0)
    source = lax.broadcasted_iota(jnp.int32, (rows, rows), 1)

    def one_slot(j, carry):
        at, length, live = slot_from[first + j], hist_len[first + j], new_len[first + j]
        moved = jnp.where(source - history < live, source - history + length, -1)
        target = jnp.where(source < history, jnp.where(source < length, source, -1), moved)
        pick = (target_row == target).astype(F32).astype(BF16)
        keys, values = [], []
        for q in range(UNITS):
            unit = early_ref[at, q].astype(F32)
            keys.append(unit[:UNIT])
            values += [unit[UNIT:], late_ref[at, q].astype(F32)]
        keys += [kv_ref[at, i, 0].astype(F32) for i in range(shards)]
        values += [kv_ref[at, i, 1].astype(F32) for i in range(shards)]
        both = [jnp.concatenate(part, axis=0).astype(BF16) for part in (keys, values)]
        placed = jnp.dot(pick, jnp.concatenate(both, axis=1), preferred_element_type=F32).astype(BF16)
        out_ref[j, 0] = placed[:, :head]
        out_ref[j, 1] = placed[:, head:]
        return carry

    lax.fori_loop(0, count, one_slot, 0, unroll=2)


def build(early, late, fresh, slot_from, hist_len, new_len):
    head = fresh.shape[4]
    rows = UNITS * UNIT + fresh.shape[1] * fresh.shape[3]
    count = slot_from.shape[0] // 4
    return pl.pallas_call(
        build_kernel,
        out_shape=jax.ShapeDtypeStruct((slot_from.shape[0], 2, rows, head), BF16),
        grid_spec=pltpu.PrefetchScalarGridSpec(
            num_scalar_prefetch=3,
            grid=(slot_from.shape[0] // count,),
            in_specs=[
                pl.BlockSpec(early.shape, lambda i, a, b, c: (0, 0, 0, 0)),
                pl.BlockSpec(late.shape, lambda i, a, b, c: (0, 0, 0, 0)),
                pl.BlockSpec(fresh.shape, lambda i, a, b, c: (0, 0, 0, 0, 0)),
            ],
            out_specs=pl.BlockSpec((count, 2, rows, head), lambda i, a, b, c: (i, 0, 0, 0)),
        ),
        compiler_params=pltpu.CompilerParams(vmem_limit_bytes=48 * 1024 * 1024),
    )(slot_from, hist_len, new_len, early, late, fresh)


def units_of(lengths):
    return (lengths + UNIT - 1) // UNIT


def run(capacity, history, new_queries, new_kv, norm_gains, ingest_source, new_owner, history_len, new_len):
    sessions, _, hist_rows, head = history.shape
    per_half = capacity // 2
    tokens, kv_heads = new_kv.shape[1], new_kv.shape[2]
    half, shard = lax.axis_index("zh"), lax.axis_index("zl")
    me = lax.axis_index(REPLICA)
    column = lax.axis_index(COLUMN)
    tie = lax.optimization_barrier
    lengths = history_len.reshape(64, sessions)

    raw_key = new_kv[:, :, :, 0, :].astype(F32)
    mean_square = jnp.mean(raw_key * raw_key, axis=-1, keepdims=True)
    normed = (raw_key * lax.rsqrt(mean_square + EPS) * norm_gains[1].astype(F32)).astype(BF16)
    fresh = jnp.stack([normed, new_kv[:, :, :, 1, :]], axis=0).transpose(3, 1, 0, 2, 4)
    fresh = with_layout_constraint(fresh, Layout(major_to_minor=(0, 1, 2, 3, 4)))

    held_units = units_of(lax.dynamic_slice(history_len, (me * sessions,), (sessions,)))
    slot = jnp.arange(capacity, dtype=jnp.int32)
    passed = jnp.cumsum(held_units)[None, :] <= slot[:, None]
    unit_session = jnp.minimum(jnp.sum(passed.astype(jnp.int32), axis=1), sessions - 1)
    unit_step = jnp.clip(slot - jnp.sum(jnp.where(passed, held_units[None, :], 0), axis=1), 0, UNITS - 1)
    key_unit = unit_session * (2 * UNITS) + unit_step
    fresh, key_unit = tie((fresh, key_unit))
    fresh_all = lax.all_gather(fresh, RING, axis=0).reshape((2, SHARDS) + fresh.shape)
    cached = history.reshape(-1, UNIT, head)
    packed_keys = jnp.take(cached, key_unit, axis=0, mode="clip")
    packed_values = jnp.take(cached, key_unit + UNITS, axis=0, mode="clip")

    source_spread = spread_index(ingest_source[replica_at(jnp.arange(64, dtype=jnp.int32))])
    source_order = source_spread.reshape(2, 32).T.reshape(64)

    def spread(part):
        return lax.all_to_all(part.reshape(64, -1, head), SPREAD, split_axis=0, concat_axis=0, tiled=True)

    def gather(pieces, rows):
        picked = jnp.take(pieces, source_order, axis=0, mode="clip").reshape(32, 2, -1, head)
        held = lax.all_to_all(picked, COLUMN, split_axis=0, concat_axis=1)
        return held.reshape(2, per_half, rows, head)

    early_part = jnp.concatenate([packed_keys, packed_values[:, : KEPT - UNIT]], axis=1)
    late_part = packed_values[:, KEPT - UNIT :]
    early_spread = spread(early_part)
    late_part, early_spread = tie((late_part, early_spread))
    late_spread = spread(late_part)
    early_held = gather(early_spread, KEPT)
    late_spread, early_held = tie((late_spread, early_held))
    late_held = gather(late_spread, 2 * UNIT - KEPT)
    early = lax.all_gather(early_held, RING, axis=0).reshape((2, SHARDS) + early_held.shape)
    late = lax.all_gather(late_held, RING, axis=0).reshape((2, SHARDS) + late_held.shape)

    owners = new_owner[:, 0].reshape(64, sessions)
    mine = ingest_source[replica_at(jnp.arange(2, dtype=jnp.int32) * 32 + column)]
    mine_owner = owners[mine]
    order = jnp.arange(sessions, dtype=jnp.int32)
    same = mine_owner[:, :, None] == mine_owner[:, None, :]
    rank = jnp.sum(jnp.logical_and(same, order[None, None, :] < order[None, :, None]), axis=2)
    target = replica_at(half * 32 + jnp.arange(32, dtype=jnp.int32))
    hit = jnp.logical_and(
        mine_owner[None, :, None, :] == target[:, None, None, None],
        rank[None, :, None, :] == jnp.arange(CAP)[None, None, :, None],
    )
    mine_units = units_of(lengths[mine])
    mine_first = jnp.cumsum(mine_units, axis=1) - mine_units
    chosen = jnp.sum(jnp.where(hit, order, 0), axis=3).reshape(32, 2 * CAP)
    chosen_first = jnp.sum(jnp.where(hit, mine_first[None, :, None, :], 0), axis=3).reshape(32, 2 * CAP)
    from_half = (jnp.arange(2 * CAP, dtype=jnp.int32) // CAP)[None, :]
    unit = jnp.minimum(chosen_first[:, :, None] + jnp.arange(UNITS, dtype=jnp.int32), capacity - 1)
    block = ((unit // per_half) * SHARDS + shard) * 2 + from_half[:, :, None]
    cached_at = (block * per_half + unit % per_half).reshape(-1)
    fresh_at = (from_half * SHARDS)[:, :, None] + jnp.arange(SHARDS, dtype=jnp.int32)
    fresh_at = ((fresh_at * kv_heads + shard) * sessions + chosen[:, :, None]).reshape(-1)

    def pack(rows, at):
        return jnp.take(rows, at, axis=0, mode="clip").reshape((32, -1) + rows.shape[1:])

    def deliver(sent):
        return lax.all_to_all(sent, COLUMN, split_axis=0, concat_axis=0, tiled=True)

    def pack_cached(part):
        return pack(part.reshape(-1, part.shape[4], head), cached_at)

    fresh_in = deliver(pack(fresh_all.reshape(-1, 2, tokens, head), fresh_at)).reshape(-1, SHARDS, 2, tokens, head)

    all_sessions = jnp.arange(64 * sessions, dtype=jnp.int32)
    owned = new_owner[:, 0] == me
    place = jnp.cumsum(owned.astype(jnp.int32)) - 1
    is_slot = jnp.logical_and(owned[None, :], place[None, :] == order[:, None])

    def of_slot(per_session):
        return jnp.sum(jnp.where(is_slot, per_session[None, :], 0), axis=1)

    slot_session = of_slot(all_sessions)
    slot_hist, slot_new = of_slot(history_len), of_slot(new_len)
    holder = slot_session // sessions
    before = jnp.concatenate([jnp.full((1,), -1, jnp.int32), holder[:-1]])
    slot_rank = (holder == before).astype(jnp.int32)
    replicas = jnp.arange(64, dtype=jnp.int32)
    ingest_at = spread_index(replicas)
    holder_hit = ingest_source[None, :] == holder[:, None]
    ingester = jnp.sum(jnp.where(holder_hit, ingest_at[None, :], 0), axis=1)
    slot_from = (ingester % 32) * (2 * CAP) + (ingester // 32) * CAP + slot_rank

    own_source = ingest_source[me]
    own_hist = lax.dynamic_slice(history_len, (own_source * sessions,), (sessions,))
    own_new = lax.dynamic_slice(new_len, (own_source * sessions,), (sessions,))
    own_first = jnp.cumsum(units_of(own_hist)) - units_of(own_hist)
    meta = jnp.stack([half, shard]).astype(jnp.int32)
    early, fresh_in = tie((early, fresh_in))
    early_in = deliver(pack_cached(early)).reshape(-1, UNITS, KEPT, head)
    weights = weigh(new_queries, early, fresh_all, norm_gains, own_hist, own_first, meta)
    late, weights = tie((late, weights))
    late_sent, early_in = tie((pack_cached(late), early_in))
    late_in = deliver(late_sent).reshape(-1, UNITS, 2 * UNIT - KEPT, head)
    attended = mix(weights, early, late, fresh_all, own_new, own_first, meta, new_queries.shape[2])
    migrated = build(early_in, late_in, fresh_in, slot_from, slot_hist, slot_new)
    return attended, migrated


def on_device(*arrays):
    history_len = arrays[6]
    sessions = arrays[0].shape[0]
    whole = sessions * UNITS
    ladder = [whole * step // 14 for step in (8, 10, 11, 14)]
    most = jnp.max(jnp.sum(units_of(history_len).reshape(64, sessions), axis=1))
    step = sum((most > room).astype(jnp.int32) for room in ladder[:-1])
    return lax.switch(step, [functools.partial(run, room) for room in ladder], *arrays)


def solution(mesh):
    split = Mesh(mesh.devices.reshape(4, 2, 4, 2, 4), ("x", "zh", "y", "core", "zl"))
    in_specs = (
        P(REPLICA, None, None, "zl"),
        P(REPLICA, "zl", None),
        P(REPLICA, "zl", None, None, None),
        P(),
        P(),
        P(),
        P(),
        P(),
    )
    out_specs = (P(REPLICA, "zl", None), P(REPLICA, None, None, "zl"))
    return jax.shard_map(on_device, mesh=split, in_specs=in_specs, out_specs=out_specs, check_vma=False)
```

```python
import functools

import jax
import jax.numpy as jnp
from jax import lax
from jax.experimental.layout import Layout, with_layout_constraint
from jax.experimental import pallas as pl
from jax.experimental.pallas import tpu as pltpu
from jax.sharding import Mesh, PartitionSpec as P

REPLICA = ("x", "zh", "y", "core")
SPREAD = ("zh", "x", "y", "core")
COLUMN = ("x", "y", "core")
RING = ("zh", "zl")
CAP = 2
SHARDS = 4
UNIT = 16
UNITS = 4
KEPT = 24
EPS = 1e-06
BF16 = jnp.bfloat16
F32 = jnp.float32


def spread_index(replica):
    x, zh, y, core = replica // 16, (replica // 8) % 2, (replica // 2) % 4, replica % 2
    return zh * 32 + x * 8 + y * 2 + core


def replica_at(spread):
    zh, x, y, core = spread // 32, (spread // 8) % 4, (spread // 2) % 4, spread % 2
    return x * 16 + zh * 8 + y * 2 + core


def fresh_rows(ref, index):
    shards = ref.shape[1]
    pieces = [ref[(0, i) + index + (0,)].astype(F32) for i in range(shards)]
    return jnp.concatenate(pieces, axis=0).astype(BF16)


def lanes_of(h, groups, head):
    return [slice((h * groups + g) * head, (h * groups + g + 1) * head) for g in range(groups)]


def unit_place(ref, first, step):
    per_half = ref.shape[3]
    at = jnp.minimum(first + step, 2 * per_half - 1)
    upper = (at >= per_half).astype(jnp.int32)
    return upper, at - upper * per_half


def weigh_kernel(meta, hist_len, unit_first, q_ref, early_ref, kv_ref, gain_ref, out_ref):
    count, tokens, width = q_ref.shape
    kv_heads, head = early_ref.shape[1], early_ref.shape[5]
    groups = width // (kv_heads * head)
    rows = groups * tokens
    fresh = kv_ref.shape[1] * tokens
    keys = out_ref.shape[2]
    history = UNITS * UNIT
    first = pl.program_id(0) * count
    gain = gain_ref[0:1, :].astype(F32)
    scale = head ** (-0.5)
    column = lax.broadcasted_iota(jnp.int32, (kv_heads * rows, keys), 1)
    token = lax.broadcasted_iota(jnp.int32, (kv_heads * rows, keys), 0) % tokens + meta[1] * tokens
    causal = jnp.logical_and(column >= history, column - history <= token)
    padding = jnp.zeros((keys - history - fresh, head), BF16)

    def one_session(s, carry):
        length = jnp.minimum(hist_len[first + s], history)
        allowed = jnp.logical_or(causal, column < length)
        places = [unit_place(early_ref, unit_first[first + s], q) for q in range(UNITS)]
        scores = []
        for h in range(kv_heads):
            query = jnp.concatenate([q_ref[s, :, lane].astype(F32) for lane in lanes_of(h, groups, head)], axis=0)
            mean_square = jnp.mean(query * query, axis=-1, keepdims=True)
            query = (query * lax.rsqrt(mean_square + EPS) * gain).astype(BF16)
            cached = [early_ref[upper, h, 0, at] for upper, at in places]
            key = jnp.concatenate(cached + [fresh_rows(kv_ref, (h, s)), padding], axis=0)
            scores.append(lax.dot_general(query, key, (((1,), (1,)), ((), ())), preferred_element_type=F32))
        scores = jnp.where(allowed, jnp.concatenate(scores, axis=0) * scale, -jnp.inf)
        weight = jnp.exp(scores - jnp.max(scores, axis=-1, keepdims=True))
        out_ref[s] = (weight * (1.0 / jnp.sum(weight, axis=-1, keepdims=True))).astype(BF16)
        return carry

    lax.fori_loop(0, count, one_session, 0, unroll=2)


def mix_kernel(meta, new_len, unit_first, w_ref, early_ref, late_ref, kv_ref, out_ref):
    count, tokens, width = out_ref.shape
    kv_heads, head = late_ref.shape[1], late_ref.shape[5]
    groups = width // (kv_heads * head)
    rows = groups * tokens
    keys = w_ref.shape[2]
    first = pl.program_id(0) * count
    fresh = kv_ref.shape[1] * tokens
    padding = jnp.zeros((keys - UNITS * UNIT - fresh, head), BF16)
    token = lax.broadcasted_iota(jnp.int32, (rows, head), 0) % tokens + meta[1] * tokens

    def one_session(s, carry):
        live = token < new_len[first + s]
        places = [unit_place(late_ref, unit_first[first + s], q) for q in range(UNITS)]
        for h in range(kv_heads):
            cached = []
            for upper, at in places:
                cached.append(early_ref[upper, h, 0, at].astype(F32)[UNIT:])
                cached.append(late_ref[upper, h, 0, at].astype(F32))
            cached = jnp.concatenate(cached, axis=0).astype(BF16)
            value = jnp.concatenate([cached, fresh_rows(kv_ref, (h, s)), padding], axis=0)
            mixed = jnp.dot(w_ref[s, h * rows : (h + 1) * rows], value, preferred_element_type=F32)
            mixed = jnp.where(live, mixed, 0.0)
            for g, lane in enumerate(lanes_of(h, groups, head)):
                out_ref[s, :, lane] = mixed[g * tokens : (g + 1) * tokens].astype(BF16)
        return carry

    lax.fori_loop(0, count, one_session, 0, unroll=2)


def units_spec(part, rows, at):
    halves, kv_heads, _, per_half, _, head = part.shape
    return pl.BlockSpec((halves, kv_heads, 1, per_half, rows, head), lambda i, m, a, b: (0, 0, m[0], 0, at, 0))


def fresh_spec(fresh, count, part):
    _, shards, kv_heads, _, _, tokens, head = fresh.shape
    return pl.BlockSpec((1, shards, kv_heads, count, 1, tokens, head), lambda i, m, a, b: (m[0], 0, 0, i, part, 0, 0))


def weigh(queries, early, fresh, gains, hist_len, unit_first, meta):
    sessions, tokens, width = queries.shape
    head = early.shape[5]
    count = sessions // 4
    columns = -(-(UNITS * UNIT + fresh.shape[1] * tokens) // 128) * 128
    whole = lambda i, m, a, b: (i, 0, 0)
    rows = width // head * tokens
    return pl.pallas_call(
        weigh_kernel,
        out_shape=jax.ShapeDtypeStruct((sessions, rows, columns), BF16),
        grid_spec=pltpu.PrefetchScalarGridSpec(
            num_scalar_prefetch=3,
            grid=(sessions // count,),
            in_specs=[
                pl.BlockSpec((count, tokens, width), whole),
                units_spec(early, UNIT, 0),
                fresh_spec(fresh, count, 0),
                pl.BlockSpec((2, head), lambda i, m, a, b: (0, 0)),
            ],
            out_specs=pl.BlockSpec((count, rows, columns), whole),
        ),
        compiler_params=pltpu.CompilerParams(vmem_limit_bytes=48 * 1024 * 1024),
    )(meta, hist_len, unit_first, queries, early, fresh, gains)


def mix(weights, early, late, fresh, new_len, unit_first, meta, width):
    sessions = weights.shape[0]
    tokens = fresh.shape[5]
    count = sessions // 4
    whole = lambda i, m, a, b: (i, 0, 0)
    return pl.pallas_call(
        mix_kernel,
        out_shape=jax.ShapeDtypeStruct((sessions, tokens, width), BF16),
        grid_spec=pltpu.PrefetchScalarGridSpec(
            num_scalar_prefetch=3,
            grid=(sessions // count,),
            in_specs=[
                pl.BlockSpec((count,) + weights.shape[1:], whole),
                units_spec(early, KEPT, 0),
                units_spec(late, late.shape[4], 0),
                fresh_spec(fresh, count, 1),
            ],
            out_specs=pl.BlockSpec((count, tokens, width), whole),
        ),
        compiler_params=pltpu.CompilerParams(vmem_limit_bytes=48 * 1024 * 1024),
    )(meta, new_len, unit_first, weights, early, late, fresh)


def build_kernel(slot_from, hist_len, new_len, early_ref, late_ref, kv_ref, out_ref):
    count, _, rows, head = out_ref.shape
    shards = kv_ref.shape[1]
    tokens = kv_ref.shape[3]
    history = rows - shards * tokens
    first = pl.program_id(0) * count
    target_row = lax.broadcasted_iota(jnp.int32, (rows, rows), 0)
    source = lax.broadcasted_iota(jnp.int32, (rows, rows), 1)

    def one_slot(j, carry):
        at, length, live = slot_from[first + j], hist_len[first + j], new_len[first + j]
        moved = jnp.where(source - history < live, source - history + length, -1)
        target = jnp.where(source < history, jnp.where(source < length, source, -1), moved)
        pick = (target_row == target).astype(F32).astype(BF16)
        keys, values = [], []
        for q in range(UNITS):
            unit = early_ref[at, q].astype(F32)
            keys.append(unit[:UNIT])
            values += [unit[UNIT:], late_ref[at, q].astype(F32)]
        keys += [kv_ref[at, i, 0].astype(F32) for i in range(shards)]
        values += [kv_ref[at, i, 1].astype(F32) for i in range(shards)]
        both = [jnp.concatenate(part, axis=0).astype(BF16) for part in (keys, values)]
        placed = jnp.dot(pick, jnp.concatenate(both, axis=1), preferred_element_type=F32).astype(BF16)
        out_ref[j, 0] = placed[:, :head]
        out_ref[j, 1] = placed[:, head:]
        return carry

    lax.fori_loop(0, count, one_slot, 0, unroll=2)


def build(early, late, fresh, slot_from, hist_len, new_len):
    head = fresh.shape[4]
    rows = UNITS * UNIT + fresh.shape[1] * fresh.shape[3]
    count = slot_from.shape[0] // 4
    return pl.pallas_call(
        build_kernel,
        out_shape=jax.ShapeDtypeStruct((slot_from.shape[0], 2, rows, head), BF16),
        grid_spec=pltpu.PrefetchScalarGridSpec(
            num_scalar_prefetch=3,
            grid=(slot_from.shape[0] // count,),
            in_specs=[
                pl.BlockSpec(early.shape, lambda i, a, b, c: (0, 0, 0, 0)),
                pl.BlockSpec(late.shape, lambda i, a, b, c: (0, 0, 0, 0)),
                pl.BlockSpec(fresh.shape, lambda i, a, b, c: (0, 0, 0, 0, 0)),
            ],
            out_specs=pl.BlockSpec((count, 2, rows, head), lambda i, a, b, c: (i, 0, 0, 0)),
        ),
        compiler_params=pltpu.CompilerParams(vmem_limit_bytes=48 * 1024 * 1024),
    )(slot_from, hist_len, new_len, early, late, fresh)


def units_of(lengths):
    return (lengths + UNIT - 1) // UNIT


def run(capacity, history, new_queries, new_kv, norm_gains, ingest_source, new_owner, history_len, new_len):
    sessions, _, hist_rows, head = history.shape
    per_half = capacity // 2
    tokens, kv_heads = new_kv.shape[1], new_kv.shape[2]
    half, shard = lax.axis_index("zh"), lax.axis_index("zl")
    me = lax.axis_index(REPLICA)
    column = lax.axis_index(COLUMN)
    tie = lax.optimization_barrier
    lengths = history_len.reshape(64, sessions)

    raw_key = new_kv[:, :, :, 0, :].astype(F32)
    mean_square = jnp.mean(raw_key * raw_key, axis=-1, keepdims=True)
    normed = (raw_key * lax.rsqrt(mean_square + EPS) * norm_gains[1].astype(F32)).astype(BF16)
    fresh = jnp.stack([normed, new_kv[:, :, :, 1, :]], axis=0).transpose(3, 1, 0, 2, 4)
    fresh = with_layout_constraint(fresh, Layout(major_to_minor=(0, 1, 2, 3, 4)))

    held_units = units_of(lax.dynamic_slice(history_len, (me * sessions,), (sessions,)))
    slot = jnp.arange(capacity, dtype=jnp.int32)
    passed = jnp.cumsum(held_units)[None, :] <= slot[:, None]
    unit_session = jnp.minimum(jnp.sum(passed.astype(jnp.int32), axis=1), sessions - 1)
    unit_step = jnp.clip(slot - jnp.sum(jnp.where(passed, held_units[None, :], 0), axis=1), 0, UNITS - 1)
    key_unit = unit_session * (2 * UNITS) + unit_step
    fresh, key_unit = tie((fresh, key_unit))
    fresh_all = lax.all_gather(fresh, RING, axis=0).reshape((2, SHARDS) + fresh.shape)
    cached = history.reshape(-1, UNIT, head)
    packed_keys = jnp.take(cached, key_unit, axis=0, mode="clip")
    packed_values = jnp.take(cached, key_unit + UNITS, axis=0, mode="clip")

    source_spread = spread_index(ingest_source[replica_at(jnp.arange(64, dtype=jnp.int32))])
    source_order = source_spread.reshape(2, 32).T.reshape(64)

    def spread(part):
        return lax.all_to_all(part.reshape(64, -1, head), SPREAD, split_axis=0, concat_axis=0, tiled=True)

    def gather(pieces, rows):
        picked = jnp.take(pieces, source_order, axis=0, mode="clip").reshape(32, 2, -1, head)
        held = lax.all_to_all(picked, COLUMN, split_axis=0, concat_axis=1)
        return held.reshape(2, per_half, rows, head)

    early_part = jnp.concatenate([packed_keys, packed_values[:, : KEPT - UNIT]], axis=1)
    late_part = packed_values[:, KEPT - UNIT :]
    early_spread = spread(early_part)
    late_part, early_spread = tie((late_part, early_spread))
    late_spread = spread(late_part)
    early_held = gather(early_spread, KEPT)
    late_spread, early_held = tie((late_spread, early_held))
    late_held = gather(late_spread, 2 * UNIT - KEPT)
    early = lax.all_gather(early_held, RING, axis=0).reshape((2, SHARDS) + early_held.shape)
    late = lax.all_gather(late_held, RING, axis=0).reshape((2, SHARDS) + late_held.shape)

    owners = new_owner[:, 0].reshape(64, sessions)
    mine = ingest_source[replica_at(jnp.arange(2, dtype=jnp.int32) * 32 + column)]
    mine_owner = owners[mine]
    order = jnp.arange(sessions, dtype=jnp.int32)
    same = mine_owner[:, :, None] == mine_owner[:, None, :]
    rank = jnp.sum(jnp.logical_and(same, order[None, None, :] < order[None, :, None]), axis=2)
    target = replica_at(half * 32 + jnp.arange(32, dtype=jnp.int32))
    hit = jnp.logical_and(
        mine_owner[None, :, None, :] == target[:, None, None, None],
        rank[None, :, None, :] == jnp.arange(CAP)[None, None, :, None],
    )
    mine_units = units_of(lengths[mine])
    mine_first = jnp.cumsum(mine_units, axis=1) - mine_units
    chosen = jnp.sum(jnp.where(hit, order, 0), axis=3).reshape(32, 2 * CAP)
    chosen_first = jnp.sum(jnp.where(hit, mine_first[None, :, None, :], 0), axis=3).reshape(32, 2 * CAP)
    from_half = (jnp.arange(2 * CAP, dtype=jnp.int32) // CAP)[None, :]
    unit = jnp.minimum(chosen_first[:, :, None] + jnp.arange(UNITS, dtype=jnp.int32), capacity - 1)
    block = ((unit // per_half) * SHARDS + shard) * 2 + from_half[:, :, None]
    cached_at = (block * per_half + unit % per_half).reshape(-1)
    fresh_at = (from_half * SHARDS)[:, :, None] + jnp.arange(SHARDS, dtype=jnp.int32)
    fresh_at = ((fresh_at * kv_heads + shard) * sessions + chosen[:, :, None]).reshape(-1)

    def pack(rows, at):
        return jnp.take(rows, at, axis=0, mode="clip").reshape((32, -1) + rows.shape[1:])

    def deliver(sent):
        return lax.all_to_all(sent, COLUMN, split_axis=0, concat_axis=0, tiled=True)

    def pack_cached(part):
        return pack(part.reshape(-1, part.shape[4], head), cached_at)

    fresh_in = deliver(pack(fresh_all.reshape(-1, 2, tokens, head), fresh_at)).reshape(-1, SHARDS, 2, tokens, head)

    all_sessions = jnp.arange(64 * sessions, dtype=jnp.int32)
    owned = new_owner[:, 0] == me
    place = jnp.cumsum(owned.astype(jnp.int32)) - 1
    is_slot = jnp.logical_and(owned[None, :], place[None, :] == order[:, None])

    def of_slot(per_session):
        return jnp.sum(jnp.where(is_slot, per_session[None, :], 0), axis=1)

    slot_session = of_slot(all_sessions)
    slot_hist, slot_new = of_slot(history_len), of_slot(new_len)
    holder = slot_session // sessions
    before = jnp.concatenate([jnp.full((1,), -1, jnp.int32), holder[:-1]])
    slot_rank = (holder == before).astype(jnp.int32)
    replicas = jnp.arange(64, dtype=jnp.int32)
    ingest_at = spread_index(replicas)
    holder_hit = ingest_source[None, :] == holder[:, None]
    ingester = jnp.sum(jnp.where(holder_hit, ingest_at[None, :], 0), axis=1)
    slot_from = (ingester % 32) * (2 * CAP) + (ingester // 32) * CAP + slot_rank

    own_source = ingest_source[me]
    own_hist = lax.dynamic_slice(history_len, (own_source * sessions,), (sessions,))
    own_new = lax.dynamic_slice(new_len, (own_source * sessions,), (sessions,))
    own_first = jnp.cumsum(units_of(own_hist)) - units_of(own_hist)
    meta = jnp.stack([half, shard]).astype(jnp.int32)
    early, fresh_in = tie((early, fresh_in))
    early_in = deliver(pack_cached(early)).reshape(-1, UNITS, KEPT, head)
    weights = weigh(new_queries, early, fresh_all, norm_gains, own_hist, own_first, meta)
    late, weights = tie((late, weights))
    late_sent, early_in = tie((pack_cached(late), early_in))
    late_in = deliver(late_sent).reshape(-1, UNITS, 2 * UNIT - KEPT, head)
    attended = mix(weights, early, late, fresh_all, own_new, own_first, meta, new_queries.shape[2])
    migrated = build(early_in, late_in, fresh_in, slot_from, slot_hist, slot_new)
    return attended, migrated


def on_device(*arrays):
    history_len = arrays[6]
    sessions = arrays[0].shape[0]
    whole = sessions * UNITS
    short = whole * 11 // 14
    most = jnp.max(jnp.sum(units_of(history_len).reshape(64, sessions), axis=1))
    return lax.cond(most <= short, functools.partial(run, short), functools.partial(run, whole), *arrays)


def solution(mesh):
    split = Mesh(mesh.devices.reshape(4, 2, 4, 2, 4), ("x", "zh", "y", "core", "zl"))
    in_specs = (
        P(REPLICA, None, None, "zl"),
        P(REPLICA, "zl", None),
        P(REPLICA, "zl", None, None, None),
        P(),
        P(),
        P(),
        P(),
        P(),
    )
    out_specs = (P(REPLICA, "zl", None), P(REPLICA, None, None, "zl"))
    return jax.shard_map(on_device, mesh=split, in_specs=in_specs, out_specs=out_specs, check_vma=False)
```
